256 devices in a mesh: region: 64 (over z, y, x_hi), mp: 4 (over x_lo, core).
Axes of the slice: x: 4 (x_hi: 2, x_lo: 2; x = x_hi * 2 + x_lo), y: 4, z: 8, core: 2. Of those that a mesh axis runs over, the one named last changes fastest.
Arguments:
- features: bfloat16 [32768, 512], P('region'), may hold values from -6 to 6
- neighbours: int32 [32768, 27], P('region'), may hold values from -1 to 1023, as said below
- order: int32 [64, 512], P('region'), may hold values from 0 to 511, each once within a row
- dest: int32 [32768, 1], P('region'), may hold values from 0 to 63; in each aligned block of 512 rows (0 to 511, 512 to 1023, ...) at most 16 rows name the same one
- conv_weight: bfloat16 [27, 512, 512], P(None, None, 'mp'), may hold values from -0.0546875 to 0.0546875
- conv_bias: float32 [512], P('mp'), may hold values from -4 to 4
- cpe_gain: float32 [512], replicated, may hold values from 0.5 to 1.5
- cpe_shift: float32 [512], replicated, may hold values from -3 to 3
- norm1_gain: float32 [512], replicated, may hold values from 0.5 to 1.5
- norm1_shift: float32 [512], replicated, may hold values from -3 to 3
- qkv_weight: bfloat16 [3, 512, 512], P(None, None, 'mp')
- proj_weight: bfloat16 [512, 512], P('mp'), may hold values from -0.25 to 0.25
- proj_bias: float32 [512], replicated, may hold values from -3 to 3
- norm2_gain: float32 [512], replicated, may hold values from 0.5 to 1.5
- norm2_shift: float32 [512], replicated, may hold values from -3 to 3
- fc1_weight: bfloat16 [512, 2048], P(None, 'mp'), may hold values from -0.25 to 0.25
- fc1_bias: float32 [2048], replicated, may hold values from -3 to 3
- fc2_weight: bfloat16 [2048, 512], P('mp'), may hold values from -0.125 to 0.125
- fc2_bias: float32 [512], replicated, may hold values from -3 to 3
Outputs:
- block_out: bfloat16 [32768, 512], P('region')
The draws below stay inside these ranges and needn't reach their ends.
Inputs may be any that keep to these rules, and one draw needn't show every extreme that they name: `neighbours`: -1 marks an absent neighbour; other values are rows of the region's points extended by 256 rows of each adjacent region, the lower region's first, and lie within 256 rows of the point's own row (256 plus its index in the region); offset 13 is the voxel itself and is never absent. Each row is an order of the region's points, every index once. `dest`: within one region's points no owner is named more than 16 times, and in every draw some region names some owner exactly 16 times.
All inputs are finite; a program needn't handle non-finite values.
Results may differ from the reference program's by a relative error of at most 0.022.
Values may be sent and summed in bfloat16 or wider, within the bound.
A program may use at most 128 MiB of HBM per device.

```python
import math
import jax
import jax.numpy as jnp
import numpy as np
from jax import lax

C = 512
HD = 16
HEADS = 32
FFN = 2048
PATCH = 1024
RIM = 256
POINTS_REG = 512
POINTS = 32768
CAP = 16
N_REGION = 64


def draw_neighbours(key, part):
    key = jax.random.fold_in(key, 11)
    reach_key, keep_key = jax.random.split(key)
    offsets = jnp.arange(27, dtype=jnp.int32)
    local_rows = jnp.arange(POINTS, dtype=jnp.int32) % POINTS_REG
    deltas = jax.random.randint(reach_key, (POINTS, 27), -RIM, RIM + 1, dtype=jnp.int32)
    deltas = jnp.where((offsets == 13)[None, :], jnp.zeros((), jnp.int32), deltas)
    first_row = (local_rows == 0)[:, None] & (offsets == 0)[None, :]
    last_row = (local_rows == POINTS_REG - 1)[:, None] & (offsets == 26)[None, :]
    deltas = jnp.where(first_row, jnp.full((), -RIM, jnp.int32), deltas)
    deltas = jnp.where(last_row, jnp.full((), RIM, jnp.int32), deltas)
    target = local_rows[:, None] + RIM + deltas
    present = jax.random.randint(keep_key, (POINTS, 27), 0, 4, dtype=jnp.int32) > 0
    present = present | (offsets == 13)[None, :] | first_row | last_row
    return jnp.where(present, target, jnp.full((), -1, jnp.int32)).astype(jnp.int32)


def draw_qkv_weight(key, part):
    key = jax.random.fold_in(key, 23)
    first = jax.random.fold_in(key, 0)
    drawn = jax.random.normal(first, (3, C, C), jnp.float32) * C ** (-0.5)
    return drawn.astype(jnp.bfloat16)


def block_scale(key, extent, cuts, least, high):
    level = 1.0
    for dim, shards_of in cuts:
        draws = jax.random.uniform(jax.random.fold_in(jax.random.fold_in(key, 6), dim), (shards_of,), jnp.float32, least / len(cuts), high / len(cuts))
        level = level * jnp.repeat(jnp.exp(draws), extent[dim] // shards_of).reshape((-1,) + (1,) * (len(extent) - 1 - dim))
    return level


def deal_out(key, own, number, rows, number_of, top, bound, lean):
    ranking = jax.random.permutation(key, number_of)
    heavy_load, usual = load_shares(number_of, rows * top, bound, lean, True), load_shares(number_of, rows * top, bound, lean, False)
    places = jnp.arange(number_of)

    def named(sizes, turn):
        used = int((sizes > 0).sum())
        fixed = max(1, used // 4)
        moved = fixed + (places - fixed + turn * (used - fixed)) % max(1, number_of - fixed)
        return jnp.zeros((number_of,), jnp.int32).at[ranking[jnp.where(places < fixed, places, moved)]].set(jnp.asarray(sizes, jnp.int32))

    sizes = jnp.where(number % 4 == 0, named(heavy_load, number // 4), named(usual, number - number // 4 - 1))
    mixed = jax.random.permutation(jax.random.fold_in(own, 3), number_of)
    donor, sink = mixed[0:number_of // 2 * 2:2], mixed[1:number_of // 2 * 2:2]
    room = jnp.minimum(sizes[donor] - 1, bound - sizes[sink]) // 2
    room = jnp.where((donor == ranking[0]) | (sink == ranking[0]) | (sizes[sink] == 0), 0, jnp.maximum(room, 0))
    moved = jax.random.randint(jax.random.fold_in(own, 4), (number_of // 2,), 0, 1 << 20) % (room + 1)
    sizes = sizes.at[donor].add(-moved).at[sink].add(moved)
    members = jnp.searchsorted(jnp.cumsum(sizes), jnp.arange(rows * top), side="right").astype(jnp.int32)
    table = members.reshape(top, rows).T
    table = table[jax.random.permutation(jax.random.fold_in(own, 1), rows)]
    turn = jax.random.randint(jax.random.fold_in(own, 2), (rows, 1), 0, top)
    return jnp.take_along_axis(table, (jnp.arange(top)[None, :] + turn) % top, axis=1)


def load_shares(count, total, most, lean, full):
    portions = [(1 << 20) // math.isqrt(grade ** lean) + 1 for grade in range(1, count + 1)]
    largest = most if full else min(most, max(-(-total // count), total * portions[0] // sum(portions)))
    least = 1 if total - largest >= count - 1 else 0
    counts, rest = [largest] + [least] * (count - 1), total - largest - least * (count - 1)
    while rest > 0:
        candidates = [i for i in range(1, count) if counts[i] < largest] or [i for i in range(1, count) if counts[i] < most]
        pool, budget = sum([portions[i] for i in candidates]), rest
        for i in candidates:
            more = min(most - counts[i], max(1, budget * portions[i] // pool), rest)
            counts[i] = counts[i] + more
            rest = rest - more
    return np.array(counts)


def normal_values(own_key, dims, spread, reach, shards=(), kind=jnp.bfloat16):
    array = jax.random.normal(own_key, dims, jnp.float32) * spread
    if len(shards) > 0:
        array = block_scale(own_key, dims, shards, -0.22, 0.18) * array
    return jnp.clip(array, min=-reach, max=reach).astype(kind)


def setup_inputs(seed: int = 0) -> dict:
    splits = jax.random.split(jax.random.key(seed), 20)
    features = normal_values(splits[0], (POINTS, C), 1.0, 6.0, ((0, 64),))
    neighbours = draw_neighbours(jax.random.fold_in(splits[19], 71), 0)
    order = jax.vmap(lambda own: jax.random.permutation(own, POINTS_REG))(jax.random.split(splits[2], N_REGION)).reshape((N_REGION, POINTS_REG)).astype(jnp.int32)
    dest_keys = jax.random.split(jax.random.fold_in(splits[3], 1), POINTS // POINTS_REG)
    dest_turns = jax.random.permutation(jax.random.fold_in(splits[3], 3), POINTS // POINTS_REG)
    dest = jax.vmap(lambda own, number: deal_out(jax.random.fold_in(splits[3], 2), own, number, POINTS_REG, N_REGION, 1, CAP, 2))(dest_keys, dest_turns).reshape((POINTS, 1))
    conv_weight = normal_values(splits[4], (27, C, C), (27 * C) ** -0.5, 0.0546875, ((2, 4),))
    conv_bias = normal_values(splits[5], (C,), 1.0, 4.0, ((0, 4),), jnp.float32)
    cpe_gain = jnp.clip(jax.random.uniform(splits[6], (C,), jnp.float32, 0.5, 1.5), 0.5, 1.5)
    cpe_shift = normal_values(splits[7], (C,), 0.5, 3.0, (), jnp.float32)
    norm1_gain = jnp.clip(jax.random.uniform(splits[8], (C,), jnp.float32, 0.5, 1.5), 0.5, 1.5)
    norm1_shift = normal_values(splits[9], (C,), 0.5, 3.0, (), jnp.float32)
    qkv_weight = draw_qkv_weight(jax.random.fold_in(splits[19], 71), 0)
    proj_weight = normal_values(splits[11], (C, C), C ** -0.5, 0.25, ((0, 4),))
    proj_bias = normal_values(splits[12], (C,), 0.5, 3.0, (), jnp.float32)
    norm2_gain = jnp.clip(jax.random.uniform(splits[13], (C,), jnp.float32, 0.5, 1.5), 0.5, 1.5)
    norm2_shift = normal_values(splits[14], (C,), 0.5, 3.0, (), jnp.float32)
    fc1_weight = normal_values(splits[15], (C, FFN), C ** -0.5, 0.25, ((1, 4),))
    fc1_bias = normal_values(splits[16], (FFN,), 0.5, 3.0, (), jnp.float32)
    fc2_weight = normal_values(splits[17], (FFN, C), FFN ** -0.5, 0.125, ((0, 4),))
    fc2_bias = normal_values(splits[18], (C,), 0.5, 3.0, (), jnp.float32)
    return {"features": features, "neighbours": neighbours, "order": order, "dest": dest, "conv_weight": conv_weight, "conv_bias": conv_bias, "cpe_gain": cpe_gain, "cpe_shift": cpe_shift, "norm1_gain": norm1_gain, "norm1_shift": norm1_shift, "qkv_weight": qkv_weight, "proj_weight": proj_weight, "proj_bias": proj_bias, "norm2_gain": norm2_gain, "norm2_shift": norm2_shift, "fc1_weight": fc1_weight, "fc1_bias": fc1_bias, "fc2_weight": fc2_weight, "fc2_bias": fc2_bias}


def layer_norm(values, scaling, shifting):
    average = lax.optimization_barrier(jnp.mean(values, axis=-1, keepdims=True))
    centred = values - average
    variance = lax.optimization_barrier(jnp.mean(centred * centred, axis=-1, keepdims=True))
    return centred * lax.rsqrt(variance + 1e-05) * scaling + shifting

def reference(features, neighbours, order, dest, conv_weight, conv_bias, cpe_gain, cpe_shift, norm1_gain, norm1_shift, qkv_weight, proj_weight, proj_bias, norm2_gain, norm2_shift, fc1_weight, fc1_bias, fc2_weight, fc2_bias):
    regions = N_REGION
    channels = C
    blocks = features.reshape(regions, POINTS_REG, channels)
    empty_rim = jnp.zeros((1, RIM, channels), features.dtype)
    before = jnp.concatenate([empty_rim, blocks[:-1, POINTS_REG - RIM:]], axis=0)
    following = jnp.concatenate([blocks[1:, :RIM], empty_rim], axis=0)
    extended = jnp.concatenate([before, blocks, following], axis=1)
    links = neighbours.reshape(regions, POINTS_REG, 27)
    flat_weight = conv_weight.reshape(27 * channels, channels)

    def convolve(pieces):
        extended_piece, link_piece = pieces
        fetched = jnp.take(extended_piece, jnp.maximum(link_piece, 0), axis=0)
        fetched = jnp.where((link_piece >= 0)[:, :, None], fetched, jnp.zeros((), fetched.dtype))
        return jnp.dot(fetched.reshape(POINTS_REG, 27 * channels), flat_weight, preferred_element_type=jnp.float32)
    conv_acc = lax.map(convolve, (extended, links))
    conv_out = (conv_acc + conv_bias).astype(jnp.bfloat16)
    cpe_x = (blocks.astype(jnp.float32) + layer_norm(conv_out.astype(jnp.float32), cpe_gain, cpe_shift)).astype(jnp.bfloat16)
    cpe_x = cpe_x.reshape(regions * POINTS_REG, channels)
    normed = layer_norm(cpe_x.astype(jnp.float32), norm1_gain, norm1_shift).astype(jnp.bfloat16)
    query = jnp.dot(normed, qkv_weight[0], preferred_element_type=jnp.float32).astype(jnp.bfloat16)
    key_all = jnp.dot(normed, qkv_weight[1], preferred_element_type=jnp.float32).astype(jnp.bfloat16)
    value = jnp.dot(normed, qkv_weight[2], preferred_element_type=jnp.float32).astype(jnp.bfloat16)
    target = dest.reshape(regions, POINTS_REG)
    sorted_target = jnp.take_along_axis(target, order, axis=1)
    owners = jnp.arange(regions, dtype=jnp.int32)
    onehot = (sorted_target[:, :, None] == owners[None, None, :]).astype(jnp.int32)
    earlier = jnp.cumsum(onehot, axis=1) - onehot
    slot_index = lax.optimization_barrier(jnp.sum(earlier * onehot, axis=2))
    buffer_rows = 2 * POINTS_REG
    source = owners[:, None]
    position = (sorted_target * buffer_rows + slot_index * regions + source).reshape(-1).astype(jnp.int32)
    source_rows = (order + source * POINTS_REG).reshape(-1).astype(jnp.int32)

    def scatter_rows(values):
        holder = jnp.zeros((regions * buffer_rows, channels), jnp.bfloat16)
        return holder.at[position].set(values[source_rows])
    query_buf = scatter_rows(query).reshape(-1, PATCH, HEADS, HD)
    key_buf = scatter_rows(key_all).reshape(-1, PATCH, HEADS, HD)
    value_buf = scatter_rows(value).reshape(-1, PATCH, HEADS, HD)
    filled = jnp.zeros((regions * buffer_rows,), jnp.float32).at[position].set(1.0).reshape(-1, PATCH)

    def attend(pieces):
        query_piece, key_piece, value_piece, live_piece = pieces
        scores = jnp.einsum('qhd,khd->hqk', query_piece.astype(jnp.float32), key_piece.astype(jnp.float32)) * HD ** (-0.5)
        scores = jnp.where(live_piece[None, None, :] > 0, scores, -1000000000.0)
        peak_score = lax.optimization_barrier(jnp.max(scores, axis=-1, keepdims=True))
        raised = jnp.exp(scores - peak_score)
        weights = (raised / lax.optimization_barrier(jnp.sum(raised, axis=-1, keepdims=True))).astype(jnp.bfloat16)
        return jnp.einsum('hqk,khd->qhd', weights.astype(jnp.float32), value_piece.astype(jnp.float32)).astype(jnp.bfloat16)
    attended_buf = lax.map(attend, (query_buf, key_buf, value_buf, filled)).reshape(-1, channels)
    attended_sorted = attended_buf[position]
    attended = jnp.zeros((regions * POINTS_REG, channels), jnp.bfloat16).at[source_rows].set(attended_sorted)
    projected = jnp.dot(attended, proj_weight, preferred_element_type=jnp.float32)
    after_attention = (cpe_x.astype(jnp.float32) + projected + proj_bias).astype(jnp.bfloat16)
    normed2 = layer_norm(after_attention.astype(jnp.float32), norm2_gain, norm2_shift).astype(jnp.bfloat16)
    hidden = jax.nn.gelu(jnp.dot(normed2, fc1_weight, preferred_element_type=jnp.float32) + fc1_bias, approximate=False).astype(jnp.bfloat16)
    lowered = jnp.dot(hidden, fc2_weight, preferred_element_type=jnp.float32)
    return (after_attention.astype(jnp.float32) + lowered + fc2_bias).astype(jnp.bfloat16)
```

```python
import functools
import jax
import jax.numpy as jnp
from jax import lax
from jax.experimental import pallas as pl
from jax.experimental.pallas import tpu as pltpu
from jax.sharding import PartitionSpec as P

HD = 16
RIM = 256
TILE = 128
WINDOW = TILE + 2 * RIM
MESH = pl.DeviceIdType.MESH
VMEM_LIMIT = 56 * 1024 * 1024
F32 = jnp.float32
BF16 = jnp.bfloat16


def iota(shape, dim, dtype=jnp.int32):
    return lax.broadcasted_iota(dtype, shape, dim)


def params(**more):
    return pltpu.CompilerParams(vmem_limit_bytes=VMEM_LIMIT, **more)


def layer_norm(values, scaling, shifting):
    average = jnp.mean(values, axis=-1, keepdims=True)
    centred = values - average
    variance = jnp.mean(centred * centred, axis=-1, keepdims=True)
    return centred * lax.rsqrt(variance + 1e-05) * scaling + shifting


def exchange(x, axis, collective_id, whole):
    count = lax.axis_size(axis)
    block = x.shape if whole else x.shape[1:]

    def kernel(x_ref, o_ref, own_sem, send_sem, recv_sem):
        me = lax.axis_index(axis)
        barrier = pltpu.get_barrier_semaphore()

        @pl.loop(1, count)
        def _(step):
            pl.semaphore_signal(
                barrier, inc=1, device_id={axis: lax.rem(me + step, count)}, device_id_type=MESH
            )

        pl.semaphore_wait(barrier, count - 1)

        def source(target):
            return x_ref if whole else x_ref.at[target]

        def copy(step, slot):
            target = lax.rem(me + step, count)
            return pltpu.make_async_remote_copy(
                src_ref=source(target),
                dst_ref=o_ref.at[slot],
                send_sem=send_sem.at[step],
                recv_sem=recv_sem.at[step],
                device_id={axis: target},
                device_id_type=MESH,
            )

        @pl.loop(1, count)
        def _(step):
            copy(step, me).start()

        own = pltpu.make_async_copy(source(me), o_ref.at[me], own_sem)
        own.start()
        own.wait()

        @pl.loop(1, count)
        def _(step):
            copy(step, lax.rem(me - step + count, count)).wait_recv()

        @pl.loop(1, count)
        def _(step):
            copy(step, me).wait_send()

    return pl.pallas_call(
        kernel,
        out_shape=jax.ShapeDtypeStruct((count,) + block, x.dtype),
        in_specs=[pl.BlockSpec(memory_space=pl.ANY)],
        out_specs=pl.BlockSpec(memory_space=pl.ANY),
        scratch_shapes=[
            pltpu.SemaphoreType.DMA,
            pltpu.SemaphoreType.DMA((count,)),
            pltpu.SemaphoreType.DMA((count,)),
        ],
        compiler_params=params(collective_id=collective_id, has_side_effects=True),
        name="exchange%d" % collective_id,
    )(x)


TAPS = 3


def conv_kernel(low_ref, mid_ref, high_ref, links_ref, w_ref, bias_ref, out_ref, ext, links, acc):
    step = pl.program_id(0)
    points, channels = mid_ref.shape
    width = out_ref.shape[1]

    @pl.when(step == 0)
    def _():
        ext[0:RIM] = low_ref[...]
        ext[RIM : RIM + points] = mid_ref[...]
        ext[RIM + points :] = high_ref[...]
        links[...] = jnp.zeros_like(links)
        links[:, 0 : links_ref.shape[1]] = links_ref[...]
        acc[...] = jnp.zeros_like(acc) + bias_ref[...]

    weight = jnp.concatenate([w_ref[k] for k in range(TAPS)], axis=1)
    lifted = jnp.dot(ext[...], weight, preferred_element_type=F32).astype(BF16)
    for tile in range(points // TILE):
        first = tile * TILE
        total = acc[first : first + TILE]
        for k in range(TAPS):
            link = links[first : first + TILE, k : k + 1] - first
            picks = (iota((TILE, WINDOW), 1) == link).astype(F32).astype(BF16)
            total += jnp.dot(
                picks,
                lifted[first : first + WINDOW, k * width : (k + 1) * width],
                preferred_element_type=F32,
            )
        acc[first : first + TILE] = total
    links[...] = pltpu.roll(links[...], links.shape[1] - TAPS, 1)

    @pl.when(step == pl.num_programs(0) - 1)
    def _():
        out_ref[...] = acc[...].astype(BF16)


def convolve(low, mid, high, links, weight, bias):
    points, channels = mid.shape
    taps, _, width = weight.shape
    full = lambda *shape: pl.BlockSpec(shape, lambda i: (0,) * len(shape))
    return pl.pallas_call(
        conv_kernel,
        grid=(taps // TAPS,),
        out_shape=jax.ShapeDtypeStruct((points, width), BF16),
        in_specs=[
            full(RIM, channels),
            full(points, channels),
            full(RIM, channels),
            full(points, taps),
            pl.BlockSpec((TAPS, channels, width), lambda i: (i, 0, 0)),
            full(1, width),
        ],
        out_specs=full(points, width),
        scratch_shapes=[
            pltpu.VMEM((points + 2 * RIM, channels), BF16),
            pltpu.VMEM((points, 128), jnp.int32),
            pltpu.VMEM((points, width), F32),
        ],
        compiler_params=params(),
        name="convolve",
    )(low, mid, high, links, weight, bias.reshape(1, width))


def route_kernel(order_ref, dest_ref, column_ref, row_ref, *, capacity):
    points = dest_ref.shape[0]
    square = (points, points)
    across, down = iota(square, 1), iota(square, 0)
    same = across == down

    def to_row(column):
        return jnp.sum(jnp.where(same, column, 0.0), axis=0, keepdims=True)

    place = jnp.sum(
        jnp.where(order_ref[...] == down, across.astype(F32), 0.0), axis=1, keepdims=True
    )
    dest = dest_ref[...].astype(F32)
    earlier = (to_row(place) < place) & (to_row(dest) == dest)
    slot = jnp.sum(jnp.where(earlier, 1.0, 0.0), axis=1, keepdims=True)
    position = dest * capacity + slot
    column_ref[...] = position.astype(jnp.int32)
    row_ref[...] = to_row(position).astype(jnp.int32)


def route(order, dest, capacity):
    points = dest.shape[0]
    return pl.pallas_call(
        functools.partial(route_kernel, capacity=capacity),
        out_shape=(
            jax.ShapeDtypeStruct((points, 1), jnp.int32),
            jax.ShapeDtypeStruct((1, points), jnp.int32),
        ),
        compiler_params=params(),
        name="route",
    )(order, dest)


def project_kernel(
    conv_ref, feat_ref, g0, b0, g1, b1, w_ref, row_ref, cpe_ref, out_ref, *, scale
):
    conv = jnp.concatenate([conv_ref[i] for i in range(conv_ref.shape[0])], axis=1).astype(F32)
    cpe = (feat_ref[...].astype(F32) + layer_norm(conv, g0[...], b0[...])).astype(BF16)
    cpe_ref[...] = cpe
    normed = layer_norm(cpe.astype(F32), g1[...], b1[...]).astype(BF16)
    weight = jnp.concatenate([w_ref[i] for i in range(3)], axis=1)
    triple = jnp.dot(normed, weight, preferred_element_type=F32).astype(BF16)
    slots, points = out_ref.shape[0], feat_ref.shape[0]
    width = w_ref.shape[2]
    rows = 256
    for first in range(0, slots, rows):
        hit = (iota((rows, points), 0) + first == row_ref[...]).astype(F32)
        filled = jnp.sum(hit, axis=1, keepdims=True) > 0
        moved = jnp.dot(hit.astype(BF16), triple, preferred_element_type=F32)
        query = jnp.where(filled, moved[:, :width] * scale, jnp.inf)
        out_ref[first : first + rows, :width] = query.astype(BF16)
        out_ref[first : first + rows, width:] = moved[:, width:].astype(BF16)


def project(conv, features, g0, b0, g1, b1, weight, row, slots):
    points, channels = features.shape
    width = weight.shape[2]
    return pl.pallas_call(
        functools.partial(project_kernel, scale=HD ** (-0.5)),
        out_shape=(
            jax.ShapeDtypeStruct((points, channels), BF16),
            jax.ShapeDtypeStruct((slots, 3 * width), BF16),
        ),
        compiler_params=params(),
        name="project",
    )(
        conv,
        features,
        g0.reshape(1, -1),
        b0.reshape(1, -1),
        g1.reshape(1, -1),
        b1.reshape(1, -1),
        weight,
        row,
    )


EMPTY_SCORE = -1e30


def attend_kernel(x_ref, out_ref, queries, keys, values):
    step = pl.program_id(0)
    rows = x_ref.shape[0]
    width = out_ref.shape[1]
    tile = out_ref.shape[0]
    heads = width // HD

    @pl.when(step == 0)
    def _():
        query = x_ref[:, :width].astype(F32)
        empty = query[:, 0:1] == jnp.inf
        one = jnp.where(iota((rows, width), 1) == 0, 1.0, 0.0)
        queries[:, :width] = jnp.where(empty, 0.0, query).astype(BF16)
        queries[:, width:] = one.astype(BF16)
        bias = jnp.where(empty, EMPTY_SCORE, 0.0) * one
        keys[:width] = x_ref[:, width : 2 * width].T
        keys[width:] = bias.T.astype(BF16)
        value = x_ref[:, 2 * width :]
        lane = iota((rows, width), 1) // HD
        for head in range(heads):
            here = jnp.where(lane == head, 1.0, 0.0).astype(BF16)
            values[head, :, :width] = value * here
            values[head, :, width:] = here

    query = queries[pl.ds(step * tile, tile)]
    lane = iota((tile, 2 * width), 1)
    total = jnp.zeros((tile, 2 * width), F32)
    for head in range(heads):
        keep = ((lane // HD) == head) | (lane >= width)
        own = query * jnp.where(keep, 1.0, 0.0).astype(BF16)
        scores = jnp.dot(own, keys[...], preferred_element_type=F32)
        peak = jnp.max(scores, axis=1, keepdims=True)
        raised = jnp.exp(scores - peak).astype(BF16)
        total += jnp.dot(raised, values[head], preferred_element_type=F32)
    out_ref[...] = (total[:, :width] / total[:, width:]).astype(BF16)


def attend(arrived, width):
    rows = arrived.shape[0]
    tile = 256
    return pl.pallas_call(
        attend_kernel,
        grid=(rows // tile,),
        out_shape=jax.ShapeDtypeStruct((rows, width), BF16),
        in_specs=[pl.BlockSpec(arrived.shape, lambda i: (0, 0))],
        out_specs=pl.BlockSpec((tile, width), lambda i: (i, 0)),
        scratch_shapes=[
            pltpu.VMEM((rows, 2 * width), BF16),
            pltpu.VMEM((2 * width, rows), BF16),
            pltpu.VMEM((width // HD, rows, 2 * width), BF16),
        ],
        compiler_params=params(),
        name="attend",
    )(arrived)


def collect_kernel(x_ref, column_ref, out_ref):
    slots, points = x_ref.shape[0], column_ref.shape[0]
    hit = (iota((points, slots), 1) == column_ref[...]).astype(F32).astype(BF16)
    moved = jnp.dot(hit, x_ref[...], preferred_element_type=F32).astype(BF16)
    rows = out_ref.shape[1]
    for part in range(out_ref.shape[0]):
        out_ref[part] = moved[part * rows : (part + 1) * rows]


def collect(returned, column, parts):
    points = column.shape[0]
    return pl.pallas_call(
        collect_kernel,
        out_shape=jax.ShapeDtypeStruct((parts, points // parts, returned.shape[1]), BF16),
        compiler_params=params(),
        name="collect",
    )(returned, column)


def finish_kernel(att_ref, cpe_ref, w_ref, bias0, g2, b2, bias1, bias2, out_ref, *, sizes):
    parts = att_ref.shape[0]
    narrow, wide = sizes
    att = jnp.concatenate([att_ref[i] for i in range(parts)], axis=1)
    proj = jnp.concatenate([w_ref[i, :narrow] for i in range(parts)], axis=0)
    after = (
        cpe_ref[...].astype(F32) + jnp.dot(att, proj, preferred_element_type=F32) + bias0[...]
    ).astype(BF16)
    normed = layer_norm(after.astype(F32), g2[...], b2[...]).astype(BF16)
    total = after.astype(F32) + bias2[...]
    for i in range(parts):
        bias = bias1[:, i * wide : (i + 1) * wide]
        raw = jnp.dot(normed, w_ref[i, narrow : narrow + wide], preferred_element_type=F32) + bias
        hidden = (0.5 * raw * (1.0 + lax.erf(raw * (0.5**0.5)))).astype(BF16)
        total += jnp.dot(hidden, w_ref[i, narrow + wide :], preferred_element_type=F32)
    out_ref[...] = total.astype(BF16)


def finish(att, cpe, weights, bias0, g2, b2, bias1, bias2, sizes):
    return pl.pallas_call(
        functools.partial(finish_kernel, sizes=sizes),
        out_shape=jax.ShapeDtypeStruct(cpe.shape, BF16),
        compiler_params=params(),
        name="finish",
    )(
        att,
        cpe,
        weights,
        bias0.reshape(1, -1),
        g2.reshape(1, -1),
        b2.reshape(1, -1),
        bias1.reshape(1, -1),
        bias2.reshape(1, -1),
    )


def neighbour_rims(features):
    count = lax.axis_size("region")
    points = features.shape[0]
    forward = [(i, i + 1) for i in range(count - 1)]
    backward = [(target, source) for source, target in forward]
    low = lax.ppermute(features[points - RIM :], "region", forward)
    high = lax.ppermute(features[:RIM], "region", backward)
    return low, high


def local(
    features,
    neighbours,
    order,
    dest,
    conv_weight,
    conv_bias,
    cpe_gain,
    cpe_shift,
    norm1_gain,
    norm1_shift,
    qkv_weight,
    proj_weight,
    proj_bias,
    norm2_gain,
    norm2_shift,
    fc1_weight,
    fc1_bias,
    fc2_weight,
    fc2_bias,
):
    points = features.shape[0]
    owners = lax.axis_size("region")
    parts = lax.axis_size("mp")
    mine = lax.axis_index("mp")
    capacity = 2 * points // owners
    slots = owners * capacity
    width = qkv_weight.shape[2]

    low, high = neighbour_rims(features)
    packed = jnp.concatenate([proj_weight, fc1_weight, fc2_weight], axis=0)
    weights = lax.all_gather(packed, "mp", axis=0)
    column, row = route(order, dest, capacity)
    conv_part = convolve(low, features, high, neighbours, conv_weight, conv_bias)
    conv = exchange(conv_part, "mp", 0, True)
    cpe, outgoing = project(
        conv, features, cpe_gain, cpe_shift, norm1_gain, norm1_shift, qkv_weight, row, slots
    )
    arrived = exchange(outgoing.reshape(owners, capacity, 3 * width), "region", 1, False)
    attended = attend(arrived.reshape(slots, 3 * width), width)
    returned = exchange(attended.reshape(owners, capacity, width), "region", 2, False)
    held = collect(returned.reshape(slots, width), column, parts)
    att = exchange(held, "mp", 3, False)
    rows = points // parts
    cpe_own = lax.dynamic_slice_in_dim(cpe, mine * rows, rows)
    own = finish(
        att,
        cpe_own,
        weights,
        proj_bias,
        norm2_gain,
        norm2_shift,
        fc1_bias,
        fc2_bias,
        (proj_weight.shape[0], fc1_weight.shape[0]),
    )
    return exchange(own, "mp", 4, True).reshape(features.shape)


def solution(mesh):
    placed = (
        P("region", None),
        P("region", None),
        P("region", None),
        P("region", None),
        P(None, None, "mp"),
        P("mp"),
        P(),
        P(),
        P(),
        P(),
        P(None, None, "mp"),
        P("mp", None),
        P(),
        P(),
        P(),
        P(None, "mp"),
        P(),
        P("mp", None),
        P(),
    )
    return jax.shard_map(
        local, mesh=mesh, in_specs=placed, out_specs=P("region", None), check_vma=False
    )
```

```python
import functools
import jax
import jax.numpy as jnp
from jax import lax
from jax.experimental import pallas as pl
from jax.experimental.pallas import tpu as pltpu
from jax.sharding import PartitionSpec as P

HD = 16
RIM = 256
TILE = 128
WINDOW = TILE + 2 * RIM
TAPS = 3
LANES = 128
EMPTY_SCORE = -1e30
MESH = pl.DeviceIdType.MESH
VMEM_LIMIT = 56 * 1024 * 1024
F32 = jnp.float32
BF16 = jnp.bfloat16


def iota(shape, dim):
    return lax.broadcasted_iota(jnp.int32, shape, dim)


def layer_norm(values, scaling, shifting):
    average = jnp.mean(values, axis=-1, keepdims=True)
    centred = values - average
    variance = jnp.mean(centred * centred, axis=-1, keepdims=True)
    return centred * lax.rsqrt(variance + 1e-05) * scaling + shifting


def route(order, dest_row, capacity):
    points = order.shape[1]
    square = (points, points)
    across, down = iota(square, 1), iota(square, 0)
    same = across == down

    def to_row(column):
        return jnp.sum(jnp.where(same, column, 0.0), axis=0, keepdims=True)

    def to_column(row):
        return jnp.sum(jnp.where(same, row, 0.0), axis=1, keepdims=True)

    place = jnp.sum(jnp.where(order == down, across.astype(F32), 0.0), axis=1, keepdims=True)
    dest_row = dest_row.astype(F32)
    dest = to_column(dest_row)
    earlier = (to_row(place) < place) & (dest_row == dest)
    slot = jnp.sum(jnp.where(earlier, 1.0, 0.0), axis=1, keepdims=True)
    position = dest * capacity + slot
    return position.astype(jnp.int32), to_row(position).astype(jnp.int32)


def kernel(
    feat_hbm, links_ref, order_ref, dest_ref, convw_hbm, convb_ref,
    g0, b0, g1, b1, qkv_ref, proj_hbm, bias0, g2, b2, fc1_hbm, bias1, fc2_hbm, bias2,
    out_ref,
    ext, links, acc, lifted, convw, gath, cpe, triple, column, row,
    outgoing, arrived, queries, keys, values, done, returned, held, att, final,
    projs, fc1s, fc2s,
    local_sem, convw_sem, halo_send, halo_recv, conv_send, conv_recv,
    points_send, points_recv, back_send, back_recv, mp_send, mp_recv,
    end_send, end_recv, wt_send, wt_recv,
):
    region, owners = lax.axis_index("region"), lax.axis_size("region")
    mine, parts = lax.axis_index("mp"), lax.axis_size("mp")
    points = feat_hbm.shape[0]
    width = convw.shape[2]
    half = points // 2
    core = lax.rem(mine, 2)
    twin = mine + 1 - 2 * core
    across = lax.rem(mine + 2, 4)
    diagonal = lax.rem(twin + 2, 4)
    above, below = lax.rem(region + 1, owners), lax.rem(region + owners - 1, owners)

    def remote(src, dst, send, recv, **target):
        return pltpu.make_async_remote_copy(
            src_ref=src, dst_ref=dst, send_sem=send, recv_sem=recv,
            device_id=target, device_id_type=MESH,
        )

    own_feat = pltpu.make_async_copy(feat_hbm, ext.at[pl.ds(RIM, points)], local_sem.at[0])
    own_feat.start()

    def weight_chunk(c):
        part = pl.ds(c * TAPS, TAPS)
        return pltpu.make_async_copy(convw_hbm.at[part], convw.at[part], convw_sem.at[c])

    chunks = convw.shape[0] // TAPS

    @pl.loop(0, chunks)
    def _(c):
        weight_chunk(c).start()

    mats = ((proj_hbm, projs), (fc1_hbm, fc1s), (fc2_hbm, fc2s))
    own_mats = [
        pltpu.make_async_copy(hbm, full.at[mine], local_sem.at[1 + i])
        for i, (hbm, full) in enumerate(mats)
    ]
    for copy in own_mats:
        copy.start()

    barrier = pltpu.get_barrier_semaphore()

    @pl.loop(1, owners)
    def _(step):
        pl.semaphore_signal(
            barrier, inc=1, device_id={"region": lax.rem(region + step, owners)},
            device_id_type=MESH,
        )

    for peer in (twin, across, diagonal):
        pl.semaphore_signal(barrier, inc=1, device_id={"mp": peer}, device_id_type=MESH)

    to_column, to_row = route(order_ref[...], dest_ref[...], outgoing.shape[2])
    column[...] = to_column
    row[...] = to_row
    padded = jnp.concatenate(
        [links_ref[...], jnp.zeros((LANES - links_ref.shape[0], points), jnp.int32)], axis=0
    )
    links[...] = padded.T
    acc[...] = jnp.zeros_like(acc) + convb_ref[...]
    pl.semaphore_wait(barrier, owners - 1 + parts - 1)

    rim_half = RIM // 2

    def low_rows(c):
        return ext.at[pl.ds(c * rim_half, rim_half)]

    def high_rows(c):
        return ext.at[pl.ds(RIM + points + c * rim_half, rim_half)]

    up = remote(
        feat_hbm.at[pl.ds(points - RIM + core * rim_half, rim_half)], low_rows(core),
        halo_send.at[0], halo_recv.at[0], region=above,
    )
    down = remote(
        feat_hbm.at[pl.ds(core * rim_half, rim_half)], high_rows(core),
        halo_send.at[1], halo_recv.at[1], region=below,
    )
    up.start()
    down.start()

    def low_forward(c):
        return remote(low_rows(c), low_rows(c), halo_send.at[2], halo_recv.at[2], mp=twin)

    def high_forward(c):
        return remote(high_rows(c), high_rows(c), halo_send.at[3], halo_recv.at[3], mp=twin)

    def lift(c, first, count, keep=None):
        weight = jnp.concatenate([convw[c * TAPS + k] for k in range(TAPS)], axis=1)
        raw = jnp.dot(ext[first : first + count], weight, preferred_element_type=F32)
        lifted[0:count] = (raw if keep is None else raw * keep).astype(BF16)

    def pick(tile, first, low, high):
        here = slice(tile * TILE, (tile + 1) * TILE)
        total = acc[here]
        for k in range(TAPS):
            hit = iota((TILE, high - low), 1) + low == links[here, k : k + 1]
            total += jnp.dot(
                hit.astype(F32).astype(BF16),
                lifted[low - first : high - first, k * width : (k + 1) * width],
                preferred_element_type=F32,
            )
        acc[here] = total

    tiles = points // TILE
    own_feat.wait()

    @pl.loop(0, chunks)
    def _(c):
        weight_chunk(c).wait()
        lift(c, RIM, points)
        for tile in range(tiles):
            low, high = max(RIM, tile * TILE), min(RIM + points, tile * TILE + WINDOW)
            pick(tile, RIM, low, high)
        links[...] = pltpu.roll(links[...], LANES - TAPS, 1)

    def gather_direct(h, peer, slot):
        return remote(
            gath.at[mine, h], gath.at[mine, h],
            conv_send.at[h, slot], conv_recv.at[h, slot], mp=peer,
        )

    def gather_arrival(h, source, slot):
        return remote(
            gath.at[source, h], gath.at[source, h],
            conv_send.at[h, slot], conv_recv.at[h, slot], mp=twin,
        )

    def send_half(h):
        gath[mine, h] = acc[h * half : (h + 1) * half].astype(BF16)
        gather_direct(h, across, 0).start()
        gather_direct(h, twin, 1).start()

    up.wait_recv()
    low_forward(core).start()
    down.wait_recv()
    high_forward(core).start()
    low_forward(1 - core).wait_recv()
    keep_low = jnp.where(region > 0, 1.0, 0.0)

    @pl.loop(0, chunks)
    def _(i):
        links[...] = pltpu.roll(links[...], TAPS, 1)
        lift(chunks - 1 - i, 0, RIM, keep_low)
        for tile in range(RIM // TILE):
            pick(tile, 0, tile * TILE, RIM)

    send_half(0)

    high_forward(1 - core).wait_recv()
    keep_high = jnp.where(region < owners - 1, 1.0, 0.0)
    end = RIM + points

    @pl.loop(0, chunks)
    def _(c):
        lift(c, end, RIM, keep_high)
        for tile in range(tiles - RIM // TILE, tiles):
            pick(tile, end, end, tile * TILE + WINDOW)
        links[...] = pltpu.roll(links[...], LANES - TAPS, 1)

    send_half(1)

    def forward_half(h):
        gather_arrival(h, across, 0).wait_recv()
        remote(
            gath.at[across, h], gath.at[across, h],
            conv_send.at[h, 2], conv_recv.at[h, 2], mp=twin,
        ).start()

    forward_half(0)

    weight_qkv = jnp.concatenate([qkv_ref[i] for i in range(3)], axis=1)
    for h in range(2):
        if h == 1:
            forward_half(1)
        gather_arrival(h, twin, 1).wait_recv()
        gather_arrival(h, diagonal, 2).wait_recv()
        here = slice(h * half, (h + 1) * half)
        conv = jnp.concatenate([gath[i, h] for i in range(parts)], axis=1).astype(F32)
        mixed = ext[RIM + h * half : RIM + (h + 1) * half].astype(F32) + layer_norm(
            conv, g0[...], b0[...]
        )
        cpe[here] = mixed.astype(BF16)
        normed = layer_norm(cpe[here].astype(F32), g1[...], b1[...]).astype(BF16)
        triple[here] = jnp.dot(normed, weight_qkv, preferred_element_type=F32).astype(BF16)

    outer, inner, capacity = outgoing.shape[0], outgoing.shape[1], outgoing.shape[2]
    group = outer * capacity
    own_outer, own_inner = region // inner, lax.rem(region, inner)

    def points_copy(a, t, target, arrival):
        other = a * inner + t
        slot = other if arrival else region
        return remote(
            outgoing.at[a, t], arrived.at[slot // inner, lax.rem(slot, inner)],
            points_send.at[target], points_recv.at[slot], region=other,
        )

    @pl.loop(0, inner)
    def _(t):
        at = iota((group, points), 0)
        slot = (at // capacity) * (inner * capacity) + t * capacity + lax.rem(at, capacity)
        hit = (slot == row[...]).astype(F32)
        filled = jnp.sum(hit, axis=1, keepdims=True) > 0
        moved = jnp.dot(hit.astype(BF16), triple[...], preferred_element_type=F32)
        query = jnp.where(filled, moved[:, :width] * HD ** (-0.5), jnp.inf).astype(BF16)
        outgoing[:, t, :, :width] = query.reshape(outer, capacity, width)
        outgoing[:, t, :, width:] = (
            moved[:, width:].astype(BF16).reshape(outer, capacity, 2 * width)
        )

        @pl.loop(0, outer)
        def _(i):
            a = lax.rem(i + own_outer, outer)
            other = a * inner + t

            @pl.when(other != region)
            def _():
                points_copy(a, t, other, False).start()

    arrived[own_outer, own_inner] = outgoing[own_outer, own_inner]

    def mat(i, part, slot, peer):
        full = mats[i][1]
        return remote(
            full.at[part], full.at[part], wt_send.at[i, slot], wt_recv.at[i, slot], mp=peer
        )

    for copy in own_mats:
        copy.wait()
    for i in range(3):
        mat(i, mine, 0, across).start()
    for i in range(3):
        mat(i, mine, 1, twin).start()

    def every_other(body):
        @pl.loop(0, owners)
        def _(s):
            @pl.when(s != region)
            def _():
                body(s)

    every_other(lambda s: points_copy(s // inner, lax.rem(s, inner), s, True).wait_recv())

    heads = width // HD
    rows = owners * capacity
    whole = arrived[...].reshape(rows, 3 * width)
    query = whole[:, :width].astype(F32)
    empty = query[:, 0:1] == jnp.inf
    one = jnp.where(iota((rows, width), 1) == 0, 1.0, 0.0)
    queries[:, :, :, :width] = (
        jnp.where(empty, 0.0, query).astype(BF16).reshape(outer, inner, capacity, width)
    )
    queries[:, :, :, width:] = one.astype(BF16).reshape(outer, inner, capacity, width)
    keys[:width] = whole[:, width : 2 * width].T
    keys[width:] = (jnp.where(empty, EMPTY_SCORE, 0.0) * one).T.astype(BF16)
    value = whole[:, 2 * width :]
    value_lane = iota((rows, width), 1) // HD
    for head in range(heads):
        here = jnp.where(value_lane == head, 1.0, 0.0).astype(BF16)
        values[head, :, :width] = value * here
        values[head, :, width:] = here

    def back_copy(a, t, target, arrival):
        other = a * inner + t
        slot = other if arrival else region
        return remote(
            done.at[a, t], returned.at[slot // inner, lax.rem(slot, inner)],
            back_send.at[target], back_recv.at[slot], region=other,
        )

    @pl.loop(0, inner)
    def _(t):
        query = queries[:, t].reshape(group, 2 * width)
        lane = iota((group, 2 * width), 1)
        total = jnp.zeros((group, 2 * width), F32)
        for head in range(heads):
            keep = ((lane // HD) == head) | (lane >= width)
            own = query * jnp.where(keep, 1.0, 0.0).astype(BF16)
            scores = jnp.dot(own, keys[...], preferred_element_type=F32)
            peak = jnp.max(scores, axis=1, keepdims=True)
            raised = jnp.exp(scores - peak).astype(BF16)
            total += jnp.dot(raised, values[head], preferred_element_type=F32)
        done[:, t] = (
            (total[:, :width] / total[:, width:]).astype(BF16).reshape(outer, capacity, width)
        )

        @pl.loop(0, outer)
        def _(i):
            a = lax.rem(i + own_outer, outer)
            other = a * inner + t

            @pl.when(other != region)
            def _():
                back_copy(a, t, other, False).start()

    returned[own_outer, own_inner] = done[own_outer, own_inner]

    for i in range(3):
        mat(i, across, 0, twin).wait_recv()
        mat(i, across, 2, twin).start()

    every_other(lambda s: back_copy(s // inner, lax.rem(s, inner), s, True).wait_recv())

    hit = (iota((points, rows), 1) == column[...]).astype(F32).astype(BF16)
    moved = jnp.dot(
        hit, returned[...].reshape(rows, width), preferred_element_type=F32
    ).astype(BF16)
    share = points // parts
    for part in range(parts):
        held[part] = moved[part * share : (part + 1) * share]

    peers = (twin, across, diagonal)

    def held_copy(i, peer, arrival):
        return remote(
            held.at[peer], att.at[peer if arrival else mine], mp_send.at[i], mp_recv.at[i], mp=peer
        )

    for i, peer in enumerate(peers):
        held_copy(i, peer, False).start()
    att[mine] = held[mine]
    for i in range(3):
        mat(i, twin, 1, twin).wait_recv()
        mat(i, diagonal, 2, twin).wait_recv()
    for i, peer in enumerate(peers):
        held_copy(i, peer, True).wait_recv()

    heads_out = jnp.concatenate([att[i] for i in range(parts)], axis=1)
    own_rows = pl.ds(pl.multiple_of(mine * share, share), share)
    after = (
        cpe[own_rows].astype(F32)
        + jnp.dot(heads_out, projs[...].reshape(points, points), preferred_element_type=F32)
        + bias0[...]
    ).astype(BF16)
    normed = layer_norm(after.astype(F32), g2[...], b2[...]).astype(BF16)
    total = after.astype(F32) + bias2[...]
    wide = fc1s.shape[2]
    for i in range(parts):
        raw = jnp.dot(normed, fc1s[i], preferred_element_type=F32)
        raw += bias1[:, i * wide : (i + 1) * wide]
        hidden = (0.5 * raw * (1.0 + lax.erf(raw * (0.5**0.5)))).astype(BF16)
        total += jnp.dot(hidden, fc2s[i], preferred_element_type=F32)
    final[mine] = total.astype(BF16)

    def end_copy(i, peer, arrival):
        slot = peer if arrival else mine
        return remote(
            final.at[slot], final.at[slot], end_send.at[i], end_recv.at[i], mp=peer
        )

    for i, peer in enumerate(peers):
        end_copy(i, peer, False).start()

    up.wait_send()
    down.wait_send()
    low_forward(core).wait_send()
    high_forward(core).wait_send()
    for h in range(2):
        for slot in range(3):
            gather_direct(h, twin, slot).wait_send()
    every_other(lambda s: points_copy(s // inner, lax.rem(s, inner), s, False).wait_send())
    every_other(lambda s: back_copy(s // inner, lax.rem(s, inner), s, False).wait_send())
    for i in range(3):
        for slot in range(3):
            mat(i, mine, slot, twin).wait_send()
    for i, peer in enumerate(peers):
        held_copy(i, peer, False).wait_send()

    for i, peer in enumerate(peers):
        end_copy(i, peer, True).wait_recv()
    for i, peer in enumerate(peers):
        end_copy(i, peer, False).wait_send()
    out_ref[...] = final[...].reshape(out_ref.shape)


def local(
    features, neighbours, order, dest, conv_weight, conv_bias,
    cpe_gain, cpe_shift, norm1_gain, norm1_shift, qkv_weight, proj_weight, proj_bias,
    norm2_gain, norm2_shift, fc1_weight, fc1_bias, fc2_weight, fc2_bias,
):
    points, channels = features.shape
    owners = lax.axis_size("region")
    parts = lax.axis_size("mp")
    capacity = 2 * points // owners
    inner = 4
    outer = owners // inner
    taps, _, width = conv_weight.shape
    rows = owners * capacity
    half = points // 2
    share = points // parts
    heads = width // HD
    wide = fc1_weight.shape[1]
    line = lambda x: x.reshape(1, -1)
    vmem = pl.BlockSpec(memory_space=pltpu.VMEM)
    hbm = pl.BlockSpec(memory_space=pl.ANY)
    blocks = (outer, inner, capacity)
    dma = pltpu.SemaphoreType.DMA
    return pl.pallas_call(
        kernel,
        out_shape=jax.ShapeDtypeStruct(features.shape, BF16),
        in_specs=[
            hbm, vmem, vmem, vmem, hbm, vmem,
            vmem, vmem, vmem, vmem, vmem, hbm, vmem, vmem, vmem, hbm, vmem, hbm, vmem,
        ],
        out_specs=vmem,
        scratch_shapes=[
            pltpu.VMEM((points + 2 * RIM, channels), BF16),
            pltpu.VMEM((points, LANES), jnp.int32),
            pltpu.VMEM((points, width), F32),
            pltpu.VMEM((points, TAPS * width), BF16),
            pltpu.VMEM((taps, channels, width), BF16),
            pltpu.VMEM((parts, 2, half, width), BF16),
            pltpu.VMEM((points, channels), BF16),
            pltpu.VMEM((points, 3 * width), BF16),
            pltpu.VMEM((points, 1), jnp.int32),
            pltpu.VMEM((1, points), jnp.int32),
            pltpu.VMEM(blocks + (3 * width,), BF16),
            pltpu.VMEM(blocks + (3 * width,), BF16),
            pltpu.VMEM(blocks + (2 * width,), BF16),
            pltpu.VMEM((2 * width, rows), BF16),
            pltpu.VMEM((heads, rows, 2 * width), BF16),
            pltpu.VMEM(blocks + (width,), BF16),
            pltpu.VMEM(blocks + (width,), BF16),
            pltpu.VMEM((parts, share, width), BF16),
            pltpu.VMEM((parts, share, width), BF16),
            pltpu.VMEM((parts, share, channels), BF16),
            pltpu.VMEM((parts,) + proj_weight.shape, BF16),
            pltpu.VMEM((parts,) + fc1_weight.shape, BF16),
            pltpu.VMEM((parts,) + fc2_weight.shape, BF16),
            dma((4,)), dma((taps // TAPS,)), dma((4,)), dma((4,)), dma((2, 3)), dma((2, 3)),
            dma((owners,)), dma((owners,)), dma((owners,)), dma((owners,)), dma((3,)), dma((3,)),
            dma((3,)), dma((3,)), dma((3, 3)), dma((3, 3)),
        ],
        compiler_params=pltpu.CompilerParams(
            collective_id=0, has_side_effects=True, vmem_limit_bytes=VMEM_LIMIT
        ),
        name="block",
    )(
        features, neighbours.T, order, dest.T, conv_weight, line(conv_bias),
        line(cpe_gain), line(cpe_shift), line(norm1_gain), line(norm1_shift), qkv_weight,
        proj_weight, line(proj_bias), line(norm2_gain), line(norm2_shift),
        fc1_weight, line(fc1_bias), fc2_weight, line(fc2_bias),
    )


def solution(mesh):
    row = P("region", None)
    placed = (
        row, row, row, row, P(None, None, "mp"), P("mp"),
        P(), P(), P(), P(), P(None, None, "mp"), P("mp", None), P(),
        P(), P(), P(None, "mp"), P(), P("mp", None), P(),
    )
    return jax.shard_map(
        local, mesh=mesh, in_specs=placed, out_specs=P("region", None), check_vma=False
    )
```

```python
import math

import jax
import jax.numpy as jnp
from jax import lax
from jax.experimental import pallas as pl
from jax.experimental.pallas import tpu as pltpu
from jax.sharding import PartitionSpec as P

HD = 16
RIM = 256
TILE = 128
WINDOW = TILE + 2 * RIM
TAPS = 9
EARLY_CHUNK = 1
LANES = 128
EMPTY_SCORE = -1e30
SCORE_SCALE = HD ** (-0.5) * math.log2(math.e)
MESH = pl.DeviceIdType.MESH
VMEM_LIMIT = 56 * 1024 * 1024
F32 = jnp.float32
BF16 = jnp.bfloat16


def iota(shape, dim):
    return lax.broadcasted_iota(jnp.int32, shape, dim)


def layer_norm(values, scaling, shifting):
    average = jnp.mean(values, axis=-1, keepdims=True)
    centred = values - average
    variance = jnp.mean(centred * centred, axis=-1, keepdims=True)
    return centred * lax.rsqrt(variance + 1e-05) * scaling + shifting


def route(order, dest_row, capacity):
    points = order.shape[1]
    square = (points, points)
    across, down = iota(square, 1), iota(square, 0)
    same = across == down

    def to_row(column):
        return jnp.sum(jnp.where(same, column, 0.0), axis=0, keepdims=True)

    def to_column(row):
        return jnp.sum(jnp.where(same, row, 0.0), axis=1, keepdims=True)

    place = jnp.sum(jnp.where(order == down, across.astype(F32), 0.0), axis=1, keepdims=True)
    dest_row = dest_row.astype(F32)
    dest = to_column(dest_row)
    earlier = (to_row(place) < place) & (dest_row == dest)
    slot = jnp.sum(jnp.where(earlier, 1.0, 0.0), axis=1, keepdims=True)
    position = dest * capacity + slot
    return position.astype(jnp.int32), to_row(position).astype(jnp.int32)


def kernel(
    feat_hbm, links_ref, order_ref, dest_ref, convw_hbm, convb_ref,
    g0, b0, g1, b1, qkv_ref, proj_hbm, bias0, g2, b2, fc1_hbm, bias1, fc2_hbm, bias2,
    out_ref,
    ext, links, acc, lifted, convw, gath, cpe, triple, column, row,
    outgoing, arrived, outgoing2, arrived2, queries, keys, values, firsts, blank, done, returned, held, att, final,
    projs, fc1s, fc2s,
    local_sem, convw_sem, halo_send, halo_recv, conv_send, conv_recv,
    points_send, points_recv, back_send, back_recv, mp_send, mp_recv,
    end_send, end_recv, wt_send, wt_recv,
):
    region, owners = lax.axis_index("region"), lax.axis_size("region")
    mine, parts = lax.axis_index("mp"), lax.axis_size("mp")
    points = feat_hbm.shape[0]
    width = convw.shape[2]
    half = points // 2
    core = lax.rem(mine, 2)
    twin = mine + 1 - 2 * core
    across = lax.rem(mine + 2, 4)
    diagonal = lax.rem(twin + 2, 4)
    above, below = lax.rem(region + 1, owners), lax.rem(region + owners - 1, owners)

    def remote(src, dst, send, recv, **target):
        return pltpu.make_async_remote_copy(
            src_ref=src, dst_ref=dst, send_sem=send, recv_sem=recv,
            device_id=target, device_id_type=MESH,
        )

    own_feat = pltpu.make_async_copy(feat_hbm, ext.at[pl.ds(RIM, points)], local_sem.at[0])
    own_feat.start()

    def weight_chunk(c):
        part = pl.ds(c * TAPS, TAPS)
        return pltpu.make_async_copy(convw_hbm.at[part], convw.at[part], convw_sem.at[c])

    chunks = convw.shape[0] // TAPS

    @pl.loop(0, chunks)
    def _(c):
        weight_chunk(c).start()

    mats = ((proj_hbm, projs), (fc1_hbm, fc1s), (fc2_hbm, fc2s))
    split = fc1s.shape[1] // 2
    pieces = (
        (projs, pl.ds(0, projs.shape[1])),
        (fc1s, pl.ds(0, split)),
        (fc1s, pl.ds(split, split)),
        (fc2s, pl.ds(0, fc2s.shape[1])),
    )
    early, late = (0, 1), (2, 3)

    def mat(i, part, slot, peer):
        full, where = pieces[i]
        return remote(
            full.at[part, where], full.at[part, where],
            wt_send.at[i, slot], wt_recv.at[i, slot], mp=peer,
        )

    def mats_out(which):
        for i in which:
            mat(i, mine, 0, across).start()
        for i in which:
            mat(i, mine, 1, twin).start()

    def mats_on(which):
        for i in which:
            mat(i, across, 0, twin).wait_recv()
            mat(i, across, 2, twin).start()

    own_mats = [
        pltpu.make_async_copy(hbm, full.at[mine], local_sem.at[1 + i])
        for i, (hbm, full) in enumerate(mats)
    ]
    for copy in own_mats:
        copy.start()

    barrier = pltpu.get_barrier_semaphore()

    @pl.loop(1, owners)
    def _(step):
        pl.semaphore_signal(
            barrier, inc=1, device_id={"region": lax.rem(region + step, owners)},
            device_id_type=MESH,
        )

    for peer in (twin, across, diagonal):
        pl.semaphore_signal(barrier, inc=1, device_id={"mp": peer}, device_id_type=MESH)

    padded = jnp.concatenate(
        [links_ref[...], jnp.zeros((LANES - links_ref.shape[0], points), jnp.int32)], axis=0
    )
    links[...] = padded.T
    acc[...] = jnp.zeros_like(acc) + convb_ref[...]
    pl.semaphore_wait(barrier, owners - 1 + parts - 1)

    rim_half = RIM // 2

    def low_rows(c):
        return ext.at[pl.ds(c * rim_half, rim_half)]

    def high_rows(c):
        return ext.at[pl.ds(RIM + points + c * rim_half, rim_half)]

    up = remote(
        feat_hbm.at[pl.ds(points - RIM + core * rim_half, rim_half)], low_rows(core),
        halo_send.at[0], halo_recv.at[0], region=above,
    )
    down = remote(
        feat_hbm.at[pl.ds(core * rim_half, rim_half)], high_rows(core),
        halo_send.at[1], halo_recv.at[1], region=below,
    )
    up.start()
    down.start()

    def low_forward(c):
        return remote(low_rows(c), low_rows(c), halo_send.at[2], halo_recv.at[2], mp=twin)

    def high_forward(c):
        return remote(high_rows(c), high_rows(c), halo_send.at[3], halo_recv.at[3], mp=twin)

    def lift(c, first, count, keep=None):
        weight = jnp.concatenate([convw[c * TAPS + k] for k in range(TAPS)], axis=1)
        raw = jnp.dot(ext[first : first + count], weight, preferred_element_type=F32)
        lifted[0:count] = (raw if keep is None else raw * keep).astype(BF16)

    def pick(tile, first, low, high):
        here = slice(tile * TILE, (tile + 1) * TILE)
        total = acc[here]
        for k in range(TAPS):
            hit = iota((TILE, high - low), 1) + low == links[here, k : k + 1]
            total += jnp.dot(
                hit.astype(F32).astype(BF16),
                lifted[low - first : high - first, k * width : (k + 1) * width],
                preferred_element_type=F32,
            )
        acc[here] = total

    tiles = points // TILE
    own_feat.wait()

    for copy in own_mats:
        copy.wait()

    @pl.loop(0, chunks)
    def _(c):
        @pl.when(c == EARLY_CHUNK)
        def _():
            mats_out(early)

        weight_chunk(c).wait()
        lift(c, RIM, points)
        for tile in range(tiles):
            low, high = max(RIM, tile * TILE), min(RIM + points, tile * TILE + WINDOW)
            pick(tile, RIM, low, high)
        links[...] = pltpu.roll(links[...], LANES - TAPS, 1)

    def gather_direct(h, peer, slot):
        return remote(
            gath.at[mine, h], gath.at[mine, h],
            conv_send.at[h, slot], conv_recv.at[h, slot], mp=peer,
        )

    def gather_arrival(h, source, slot):
        return remote(
            gath.at[source, h], gath.at[source, h],
            conv_send.at[h, slot], conv_recv.at[h, slot], mp=twin,
        )

    def send_half(h):
        gath[mine, h] = acc[h * half : (h + 1) * half].astype(BF16)
        gather_direct(h, across, 0).start()
        gather_direct(h, twin, 1).start()

    up.wait_recv()
    low_forward(core).start()
    down.wait_recv()
    high_forward(core).start()
    low_forward(1 - core).wait_recv()
    keep_low = jnp.where(region > 0, 1.0, 0.0)

    @pl.loop(0, chunks)
    def _(i):
        links[...] = pltpu.roll(links[...], TAPS, 1)
        lift(chunks - 1 - i, 0, RIM, keep_low)
        for tile in range(RIM // TILE):
            pick(tile, 0, tile * TILE, RIM)

    send_half(0)

    high_forward(1 - core).wait_recv()
    keep_high = jnp.where(region < owners - 1, 1.0, 0.0)
    end = RIM + points

    @pl.loop(0, chunks)
    def _(c):
        lift(c, end, RIM, keep_high)
        for tile in range(tiles - RIM // TILE, tiles):
            pick(tile, end, end, tile * TILE + WINDOW)
        links[...] = pltpu.roll(links[...], LANES - TAPS, 1)

    send_half(1)

    def forward_half(h):
        gather_arrival(h, across, 0).wait_recv()
        remote(
            gath.at[across, h], gath.at[across, h],
            conv_send.at[h, 2], conv_recv.at[h, 2], mp=twin,
        ).start()

    forward_half(0)

    to_column, to_row = route(order_ref[...], dest_ref[...], outgoing.shape[2])
    column[...] = to_column
    row[...] = to_row
    forward_half(1)

    weight_qkv = jnp.concatenate([qkv_ref[i] for i in range(3)], axis=1)
    for h in range(2):
        gather_arrival(h, twin, 1).wait_recv()
        gather_arrival(h, diagonal, 2).wait_recv()
        here = slice(h * half, (h + 1) * half)
        conv = jnp.concatenate([gath[i, h] for i in range(parts)], axis=1).astype(F32)
        mixed = ext[RIM + h * half : RIM + (h + 1) * half].astype(F32) + layer_norm(
            conv, g0[...], b0[...]
        )
        cpe[here] = mixed.astype(BF16)
        normed = layer_norm(cpe[here].astype(F32), g1[...], b1[...]).astype(BF16)
        raw = jnp.dot(normed, weight_qkv, preferred_element_type=F32)
        query = (raw[:, :width] * SCORE_SCALE).astype(BF16)
        key = raw[:, width : 2 * width].astype(BF16)
        side = width // 2
        triple[here, :width] = jnp.concatenate([query[:, :side], key[:, :side]], axis=1)
        triple[here, width : 2 * width] = raw[:, 2 * width :].astype(BF16)
        triple[here, 2 * width :] = jnp.concatenate([query[:, side:], key[:, side:]], axis=1)

    outer, inner, capacity = outgoing.shape[0], outgoing.shape[1], outgoing.shape[2]
    group = outer * capacity
    own_outer, own_inner = region // inner, lax.rem(region, inner)

    def points_copy(first, a, t, target, arrival):
        other = a * inner + t
        slot = other if arrival else region
        src, dst = (outgoing, arrived) if first else (outgoing2, arrived2)
        kind = 0 if first else 1
        return remote(
            src.at[a, t], dst.at[slot // inner, lax.rem(slot, inner)],
            points_send.at[kind, target], points_recv.at[kind, slot], region=other,
        )

    def points_out(first, t):
        @pl.loop(0, outer)
        def _(i):
            a = lax.rem(i + own_outer, outer)
            other = a * inner + t

            @pl.when(other != region)
            def _():
                points_copy(first, a, t, other, False).start()

    @pl.loop(0, inner)
    def _(t):
        at = iota((group, points), 0)
        slot = (at // capacity) * (inner * capacity) + t * capacity + lax.rem(at, capacity)
        hit = (slot == row[...]).astype(F32)
        filled = jnp.sum(hit, axis=1, keepdims=True) > 0
        moved = jnp.dot(hit.astype(BF16), triple[...], preferred_element_type=F32)
        pair = jnp.where(filled, moved[:, :width], jnp.inf).astype(BF16)
        outgoing[:, t, :, :width] = pair.reshape(outer, capacity, width)
        outgoing[:, t, :, width:] = (
            moved[:, width : 2 * width].astype(BF16).reshape(outer, capacity, width)
        )
        outgoing2[:, t] = moved[:, 2 * width :].astype(BF16).reshape(outer, capacity, width)
        points_out(True, t)

    @pl.loop(0, inner)
    def _(t):
        points_out(False, t)

    arrived[own_outer, own_inner] = outgoing[own_outer, own_inner]
    arrived2[own_outer, own_inner] = outgoing2[own_outer, own_inner]

    mats_out(late)
    mats_on(early)

    def every_other(body):
        @pl.loop(0, owners)
        def _(s):
            @pl.when(s != region)
            def _():
                body(s)

    heads = width // HD
    rows = owners * capacity
    side = width // 2
    near = heads // 2

    def prepare(kind, pairs, empty):
        lane = iota((rows, width), 1)
        marked = jnp.where(lane == side, 1.0, 0.0)
        pairs = jnp.where(empty, 0.0, pairs.astype(F32))
        query = jnp.where(lane < side, pairs, marked)
        queries[kind] = query.astype(BF16).reshape(inner, group, width)
        key = jnp.where(lane < side, pltpu.roll(pairs, side, 1), marked * bias_of(empty))
        keys[kind] = key.astype(BF16).T

    def bias_of(empty):
        return jnp.where(empty, EMPTY_SCORE, 0.0)

    every_other(
        lambda s: points_copy(True, s // inner, lax.rem(s, inner), s, True).wait_recv()
    )
    whole = jnp.concatenate([arrived[:, t].reshape(group, 2 * width) for t in range(inner)], axis=0)
    empty = whole[:, 0:1].astype(F32) == jnp.inf
    prepare(0, whole[:, :width], empty)
    blank[...] = jnp.where(empty, 1.0, 0.0)
    value = whole[:, width:]
    value_lane = iota((rows, width), 1) // HD
    for head in range(heads):
        mask = jnp.where(value_lane == head, 1.0, 0.0).astype(BF16)
        values[head, :, :width] = value * mask
        values[head, :, width:] = mask

    def attend(kind, t):
        query = queries[kind, t]
        lane = iota((group, width), 1)
        total = jnp.zeros((group, 2 * width), F32)
        for head in range(near):
            keep = ((lane // HD) == head) | (lane >= side)
            own = query * jnp.where(keep, 1.0, 0.0).astype(BF16)
            scores = jnp.dot(own, keys[kind], preferred_element_type=F32)
            peak = jnp.max(scores, axis=1, keepdims=True)
            raised = jnp.exp2(scores - peak).astype(BF16)
            total += jnp.dot(raised, values[kind * near + head], preferred_element_type=F32)
        here = (lane // side) == kind
        return jnp.where(here, total[:, :width] / jnp.where(here, total[:, width:], 1.0), 0.0)

    @pl.loop(0, inner)
    def _(t):
        firsts[t] = attend(0, t)

    every_other(
        lambda s: points_copy(False, s // inner, lax.rem(s, inner), s, True).wait_recv()
    )
    prepare(
        1,
        jnp.concatenate([arrived2[:, t].reshape(group, width) for t in range(inner)], axis=0),
        blank[...] > 0,
    )

    def back_copy(a, t, target, arrival):
        other = a * inner + t
        slot = other if arrival else region
        return remote(
            done.at[a, t], returned.at[slot // inner, lax.rem(slot, inner)],
            back_send.at[target], back_recv.at[slot], region=other,
        )

    @pl.loop(0, inner)
    def _(t):
        done[:, t] = (firsts[t] + attend(1, t)).astype(BF16).reshape(outer, capacity, width)

        @pl.loop(0, outer)
        def _(i):
            a = lax.rem(i + own_outer, outer)
            other = a * inner + t

            @pl.when(other != region)
            def _():
                back_copy(a, t, other, False).start()

    returned[own_outer, own_inner] = done[own_outer, own_inner]

    mats_on(late)

    every_other(lambda s: back_copy(s // inner, lax.rem(s, inner), s, True).wait_recv())

    hit = (iota((points, rows), 1) == column[...]).astype(F32).astype(BF16)
    moved = jnp.dot(
        hit, returned[...].reshape(rows, width), preferred_element_type=F32
    ).astype(BF16)
    share = points // parts
    for part in range(parts):
        held[part] = moved[part * share : (part + 1) * share]

    peers = (twin, across, diagonal)

    def held_copy(i, peer, arrival):
        return remote(
            held.at[peer], att.at[peer if arrival else mine], mp_send.at[i], mp_recv.at[i], mp=peer
        )

    for i, peer in enumerate(peers):
        held_copy(i, peer, False).start()
    att[mine] = held[mine]
    for i in range(4):
        mat(i, twin, 1, twin).wait_recv()
        mat(i, diagonal, 2, twin).wait_recv()
    for i, peer in enumerate(peers):
        held_copy(i, peer, True).wait_recv()

    heads_out = jnp.concatenate([att[i] for i in range(parts)], axis=1)
    own_rows = pl.ds(pl.multiple_of(mine * share, share), share)
    after = (
        cpe[own_rows].astype(F32)
        + jnp.dot(heads_out, projs[...].reshape(points, points), preferred_element_type=F32)
        + bias0[...]
    ).astype(BF16)
    normed = layer_norm(after.astype(F32), g2[...], b2[...]).astype(BF16)
    total = after.astype(F32) + bias2[...]
    wide = fc1s.shape[2]
    for i in range(parts):
        raw = jnp.dot(normed, fc1s[i], preferred_element_type=F32)
        raw += bias1[:, i * wide : (i + 1) * wide]
        hidden = (0.5 * raw * (1.0 + lax.erf(raw * (0.5**0.5)))).astype(BF16)
        total += jnp.dot(hidden, fc2s[i], preferred_element_type=F32)
    final[mine] = total.astype(BF16)

    part_rows = share // 2

    def end_copy(part, piece, slot, peer):
        where = pl.ds(piece * part_rows, part_rows)
        return remote(
            final.at[part, where], final.at[part, where],
            end_send.at[piece, slot], end_recv.at[piece, slot], mp=peer,
        )

    for piece in range(2):
        end_copy(mine, piece, 0, across).start()
    for piece in range(2):
        end_copy(mine, piece, 1, twin).start()
    for piece in range(2):
        end_copy(across, piece, 0, twin).wait_recv()
        end_copy(across, piece, 2, twin).start()

    up.wait_send()
    down.wait_send()
    low_forward(core).wait_send()
    high_forward(core).wait_send()
    for h in range(2):
        for slot in range(3):
            gather_direct(h, twin, slot).wait_send()
    for first in (True, False):
        every_other(
            lambda s: points_copy(first, s // inner, lax.rem(s, inner), s, False).wait_send()
        )
    every_other(lambda s: back_copy(s // inner, lax.rem(s, inner), s, False).wait_send())
    for i in range(4):
        for slot in range(3):
            mat(i, mine, slot, twin).wait_send()
    for i, peer in enumerate(peers):
        held_copy(i, peer, False).wait_send()

    for piece in range(2):
        end_copy(twin, piece, 1, twin).wait_recv()
        end_copy(diagonal, piece, 2, twin).wait_recv()
    for piece in range(2):
        for slot in range(3):
            end_copy(mine, piece, slot, twin).wait_send()
    out_ref[...] = final[...].reshape(out_ref.shape)


def local(
    features, neighbours, order, dest, conv_weight, conv_bias,
    cpe_gain, cpe_shift, norm1_gain, norm1_shift, qkv_weight, proj_weight, proj_bias,
    norm2_gain, norm2_shift, fc1_weight, fc1_bias, fc2_weight, fc2_bias,
):
    points, channels = features.shape
    owners = lax.axis_size("region")
    parts = lax.axis_size("mp")
    capacity = 2 * points // owners
    inner = 4
    outer = owners // inner
    taps, _, width = conv_weight.shape
    rows = owners * capacity
    half = points // 2
    share = points // parts
    heads = width // HD
    wide = fc1_weight.shape[1]
    line = lambda x: x.reshape(1, -1)
    vmem = pl.BlockSpec(memory_space=pltpu.VMEM)
    hbm = pl.BlockSpec(memory_space=pl.ANY)
    blocks = (outer, inner, capacity)
    dma = pltpu.SemaphoreType.DMA
    return pl.pallas_call(
        kernel,
        out_shape=jax.ShapeDtypeStruct(features.shape, BF16),
        in_specs=[
            hbm, vmem, vmem, vmem, hbm, vmem,
            vmem, vmem, vmem, vmem, vmem, hbm, vmem, vmem, vmem, hbm, vmem, hbm, vmem,
        ],
        out_specs=vmem,
        scratch_shapes=[
            pltpu.VMEM((points + 2 * RIM, channels), BF16),
            pltpu.VMEM((points, LANES), jnp.int32),
            pltpu.VMEM((points, width), F32),
            pltpu.VMEM((points, TAPS * width), BF16),
            pltpu.VMEM((taps, channels, width), BF16),
            pltpu.VMEM((parts, 2, half, width), BF16),
            pltpu.VMEM((points, channels), BF16),
            pltpu.VMEM((points, 3 * width), BF16),
            pltpu.VMEM((points, 1), jnp.int32),
            pltpu.VMEM((1, points), jnp.int32),
            pltpu.VMEM(blocks + (2 * width,), BF16),
            pltpu.VMEM(blocks + (2 * width,), BF16),
            pltpu.VMEM(blocks + (width,), BF16),
            pltpu.VMEM(blocks + (width,), BF16),
            pltpu.VMEM((2, inner, outer * capacity, width), BF16),
            pltpu.VMEM((2, width, rows), BF16),
            pltpu.VMEM((heads, rows, 2 * width), BF16),
            pltpu.VMEM((inner, outer * capacity, width), F32),
            pltpu.VMEM((rows, 1), F32),
            pltpu.VMEM(blocks + (width,), BF16),
            pltpu.VMEM(blocks + (width,), BF16),
            pltpu.VMEM((parts, share, width), BF16),
            pltpu.VMEM((parts, share, width), BF16),
            pltpu.VMEM((parts, share, channels), BF16),
            pltpu.VMEM((parts,) + proj_weight.shape, BF16),
            pltpu.VMEM((parts,) + fc1_weight.shape, BF16),
            pltpu.VMEM((parts,) + fc2_weight.shape, BF16),
            dma((4,)), dma((taps // TAPS,)), dma((4,)), dma((4,)), dma((2, 3)), dma((2, 3)),
            dma((2, owners)), dma((2, owners)), dma((owners,)), dma((owners,)), dma((3,)), dma((3,)),
            dma((2, 3)), dma((2, 3)), dma((4, 3)), dma((4, 3)),
        ],
        compiler_params=pltpu.CompilerParams(
            collective_id=0, has_side_effects=True, vmem_limit_bytes=VMEM_LIMIT
        ),
        name="block",
    )(
        features, neighbours.T, order, dest.T, conv_weight, line(conv_bias),
        line(cpe_gain), line(cpe_shift), line(norm1_gain), line(norm1_shift), qkv_weight,
        proj_weight, line(proj_bias), line(norm2_gain), line(norm2_shift),
        fc1_weight, line(fc1_bias), fc2_weight, line(fc2_bias),
    )


def solution(mesh):
    row = P("region", None)
    placed = (
        row, row, row, row, P(None, None, "mp"), P("mp"),
        P(), P(), P(), P(), P(None, None, "mp"), P("mp", None), P(),
        P(), P(), P(None, "mp"), P(), P("mp", None), P(),
    )
    return jax.shard_map(
        local, mesh=mesh, in_specs=placed, out_specs=P("region", None), check_vma=False
    )
```

```python
import math

import jax
import jax.numpy as jnp
from jax import lax
from jax.experimental import pallas as pl
from jax.experimental.pallas import tpu as pltpu
from jax.sharding import PartitionSpec as P

HD = 16
RIM = 256
TILE = 128
WINDOW = TILE + 2 * RIM
TAPS = 9
LANES = 128
EMPTY_SCORE = -1e30
SCORE_SCALE = HD ** (-0.5) * math.log2(math.e)
MESH = pl.DeviceIdType.MESH
VMEM_LIMIT = 56 * 1024 * 1024
F32 = jnp.float32
BF16 = jnp.bfloat16


def iota(shape, dim):
    return lax.broadcasted_iota(jnp.int32, shape, dim)


def layer_norm(values, scaling, shifting):
    average = jnp.mean(values, axis=-1, keepdims=True)
    centred = values - average
    variance = jnp.mean(centred * centred, axis=-1, keepdims=True)
    return centred * lax.rsqrt(variance + 1e-05) * scaling + shifting


def route(order, dest_row, capacity):
    points = order.shape[1]
    square = (points, points)
    across, down = iota(square, 1), iota(square, 0)
    same = across == down

    def to_row(column):
        return jnp.sum(jnp.where(same, column, 0.0), axis=0, keepdims=True)

    def to_column(row):
        return jnp.sum(jnp.where(same, row, 0.0), axis=1, keepdims=True)

    place = jnp.sum(jnp.where(order == down, across.astype(F32), 0.0), axis=1, keepdims=True)
    dest_row = dest_row.astype(F32)
    dest = to_column(dest_row)
    earlier = (to_row(place) < place) & (dest_row == dest)
    slot = jnp.sum(jnp.where(earlier, 1.0, 0.0), axis=1, keepdims=True)
    position = dest * capacity + slot
    return position.astype(jnp.int32), to_row(position).astype(jnp.int32)


def kernel(
    feat_hbm, links_ref, order_ref, dest_ref, convw_hbm, convb_ref,
    g0, b0, g1, b1, qkv_ref, proj_hbm, bias0, g2, b2, fc1_hbm, bias1, fc2_hbm, bias2,
    out_ref,
    ext, links, acc, lifted, convw, gath, cpe, triple, column, row,
    outgoing, arrived, outgoing2, arrived2, queries, keys, values, firsts, blank, collecting, done, returned, held, att, final,
    projs, fc1s, fc2s,
    local_sem, convw_sem, halo_send, halo_recv, conv_send, conv_recv,
    points_send, points_recv, back_send, back_recv, mp_send, mp_recv,
    end_send, end_recv, wt_send, wt_recv,
):
    region, owners = lax.axis_index("region"), lax.axis_size("region")
    mine, parts = lax.axis_index("mp"), lax.axis_size("mp")
    points = feat_hbm.shape[0]
    width = convw.shape[2]
    half = points // 2
    core = lax.rem(mine, 2)
    twin = mine + 1 - 2 * core
    across = lax.rem(mine + 2, 4)
    diagonal = lax.rem(twin + 2, 4)
    above, below = lax.rem(region + 1, owners), lax.rem(region + owners - 1, owners)

    def remote(src, dst, send, recv, **target):
        return pltpu.make_async_remote_copy(
            src_ref=src, dst_ref=dst, send_sem=send, recv_sem=recv,
            device_id=target, device_id_type=MESH,
        )

    own_feat = pltpu.make_async_copy(feat_hbm, ext.at[pl.ds(RIM, points)], local_sem.at[0])
    own_feat.start()

    def weight_chunk(c):
        part = pl.ds(c * TAPS, TAPS)
        return pltpu.make_async_copy(convw_hbm.at[part], convw.at[part], convw_sem.at[c])

    chunks = convw.shape[0] // TAPS

    @pl.loop(0, chunks)
    def _(c):
        weight_chunk(c).start()

    mats = ((proj_hbm, projs), (fc1_hbm, fc1s), (fc2_hbm, fc2s))
    split = fc1s.shape[1] // 2
    pieces = (
        (projs, pl.ds(0, projs.shape[1])),
        (fc1s, pl.ds(0, split)),
        (fc1s, pl.ds(split, split)),
        (fc2s, pl.ds(0, fc2s.shape[1])),
    )
    early, late = (0, 1), (2, 3)

    def mat(i, part, slot, peer):
        full, where = pieces[i]
        return remote(
            full.at[part, where], full.at[part, where],
            wt_send.at[i, slot], wt_recv.at[i, slot], mp=peer,
        )

    def mats_out(which):
        for i in which:
            mat(i, mine, 0, across).start()
        for i in which:
            mat(i, mine, 1, twin).start()

    def mats_on(which):
        for i in which:
            mat(i, across, 0, twin).wait_recv()
            mat(i, across, 2, twin).start()

    own_mats = [
        pltpu.make_async_copy(hbm, full.at[mine], local_sem.at[1 + i])
        for i, (hbm, full) in enumerate(mats)
    ]
    for copy in own_mats:
        copy.start()

    barrier = pltpu.get_barrier_semaphore()

    @pl.loop(1, owners)
    def _(step):
        pl.semaphore_signal(
            barrier, inc=1, device_id={"region": lax.rem(region + step, owners)},
            device_id_type=MESH,
        )

    for peer in (twin, across, diagonal):
        pl.semaphore_signal(barrier, inc=1, device_id={"mp": peer}, device_id_type=MESH)

    padded = jnp.concatenate(
        [links_ref[...], jnp.zeros((LANES - links_ref.shape[0], points), jnp.int32)], axis=0
    )
    links[...] = padded.T
    acc[...] = jnp.zeros_like(acc) + convb_ref[...]
    pl.semaphore_wait(barrier, owners - 1 + parts - 1)

    rim_half = RIM // 2

    def low_rows(c):
        return ext.at[pl.ds(c * rim_half, rim_half)]

    def high_rows(c):
        return ext.at[pl.ds(RIM + points + c * rim_half, rim_half)]

    up = remote(
        feat_hbm.at[pl.ds(points - RIM + core * rim_half, rim_half)], low_rows(core),
        halo_send.at[0], halo_recv.at[0], region=above,
    )
    down = remote(
        feat_hbm.at[pl.ds(core * rim_half, rim_half)], high_rows(core),
        halo_send.at[1], halo_recv.at[1], region=below,
    )
    up.start()
    down.start()

    def low_forward(c):
        return remote(low_rows(c), low_rows(c), halo_send.at[2], halo_recv.at[2], mp=twin)

    def high_forward(c):
        return remote(high_rows(c), high_rows(c), halo_send.at[3], halo_recv.at[3], mp=twin)

    def lift(c, first, count, keep=None):
        weight = jnp.concatenate([convw[c * TAPS + k] for k in range(TAPS)], axis=1)
        raw = jnp.dot(ext[first : first + count], weight, preferred_element_type=F32)
        lifted[0:count] = (raw if keep is None else raw * keep).astype(BF16)

    def pick(tile, first, low, high):
        here = slice(tile * TILE, (tile + 1) * TILE)
        total = acc[here]
        for k in range(TAPS):
            hit = iota((TILE, high - low), 1) + low == links[here, k : k + 1]
            total += jnp.dot(
                hit.astype(F32).astype(BF16),
                lifted[low - first : high - first, k * width : (k + 1) * width],
                preferred_element_type=F32,
            )
        acc[here] = total

    tiles = points // TILE
    own_feat.wait()

    for copy in own_mats:
        copy.wait()

    @pl.loop(0, chunks)
    def _(c):
        weight_chunk(c).wait()
        lift(c, RIM, points)
        for tile in range(tiles):
            low, high = max(RIM, tile * TILE), min(RIM + points, tile * TILE + WINDOW)
            pick(tile, RIM, low, high)
        links[...] = pltpu.roll(links[...], LANES - TAPS, 1)

    def gather_direct(h, peer, slot):
        return remote(
            gath.at[mine, h], gath.at[mine, h],
            conv_send.at[h, slot], conv_recv.at[h, slot], mp=peer,
        )

    def gather_arrival(h, source, slot):
        return remote(
            gath.at[source, h], gath.at[source, h],
            conv_send.at[h, slot], conv_recv.at[h, slot], mp=twin,
        )

    def send_half(h):
        gath[mine, h] = acc[h * half : (h + 1) * half].astype(BF16)
        gather_direct(h, across, 0).start()
        gather_direct(h, twin, 1).start()

    up.wait_recv()
    low_forward(core).start()
    down.wait_recv()
    high_forward(core).start()
    low_forward(1 - core).wait_recv()
    keep_low = jnp.where(region > 0, 1.0, 0.0)

    @pl.loop(0, chunks)
    def _(i):
        links[...] = pltpu.roll(links[...], TAPS, 1)
        lift(chunks - 1 - i, 0, RIM, keep_low)
        for tile in range(RIM // TILE):
            pick(tile, 0, tile * TILE, RIM)

    send_half(0)

    high_forward(1 - core).wait_recv()
    keep_high = jnp.where(region < owners - 1, 1.0, 0.0)
    end = RIM + points

    @pl.loop(0, chunks)
    def _(c):
        lift(c, end, RIM, keep_high)
        for tile in range(tiles - RIM // TILE, tiles):
            pick(tile, end, end, tile * TILE + WINDOW)
        links[...] = pltpu.roll(links[...], LANES - TAPS, 1)

    send_half(1)

    def forward_half(h):
        gather_arrival(h, across, 0).wait_recv()
        remote(
            gath.at[across, h], gath.at[across, h],
            conv_send.at[h, 2], conv_recv.at[h, 2], mp=twin,
        ).start()

    forward_half(0)

    to_column, to_row = route(order_ref[...], dest_ref[...], outgoing.shape[2])
    column[...] = to_column
    row[...] = to_row
    forward_half(1)

    weight_qkv = jnp.concatenate([qkv_ref[i] for i in range(3)], axis=1)
    for h in range(2):
        gather_arrival(h, twin, 1).wait_recv()
        gather_arrival(h, diagonal, 2).wait_recv()
        here = slice(h * half, (h + 1) * half)
        conv = jnp.concatenate([gath[i, h] for i in range(parts)], axis=1).astype(F32)
        mixed = ext[RIM + h * half : RIM + (h + 1) * half].astype(F32) + layer_norm(
            conv, g0[...], b0[...]
        )
        cpe[here] = mixed.astype(BF16)
        normed = layer_norm(cpe[here].astype(F32), g1[...], b1[...]).astype(BF16)
        raw = jnp.dot(normed, weight_qkv, preferred_element_type=F32)
        query = (raw[:, :width] * SCORE_SCALE).astype(BF16)
        key = raw[:, width : 2 * width].astype(BF16)
        side = width // 2
        triple[here, :width] = jnp.concatenate([query[:, :side], key[:, :side]], axis=1)
        triple[here, width : 2 * width] = raw[:, 2 * width :].astype(BF16)
        triple[here, 2 * width :] = jnp.concatenate([query[:, side:], key[:, side:]], axis=1)

    outer, inner, capacity = outgoing.shape[0], outgoing.shape[1], outgoing.shape[2]
    group = outer * capacity
    own_outer, own_inner = region // inner, lax.rem(region, inner)

    def points_copy(first, a, t, target, arrival):
        other = a * inner + t
        slot = other if arrival else region
        src, dst = (outgoing, arrived) if first else (outgoing2, arrived2)
        kind = 0 if first else 1
        return remote(
            src.at[a, t], dst.at[slot // inner, lax.rem(slot, inner)],
            points_send.at[kind, target], points_recv.at[kind, slot], region=other,
        )

    def points_out(first, t):
        @pl.loop(0, outer)
        def _(i):
            a = lax.rem(i + own_outer, outer)
            other = a * inner + t

            @pl.when(other != region)
            def _():
                points_copy(first, a, t, other, False).start()

    @pl.loop(0, inner)
    def _(t):
        at = iota((group, points), 0)
        slot = (at // capacity) * (inner * capacity) + t * capacity + lax.rem(at, capacity)
        hit = (slot == row[...]).astype(F32)
        filled = jnp.sum(hit, axis=1, keepdims=True) > 0
        moved = jnp.dot(hit.astype(BF16), triple[...], preferred_element_type=F32)
        pair = jnp.where(filled, moved[:, :width], jnp.inf).astype(BF16)
        outgoing[:, t, :, :width] = pair.reshape(outer, capacity, width)
        outgoing[:, t, :, width:] = (
            moved[:, width : 2 * width].astype(BF16).reshape(outer, capacity, width)
        )
        outgoing2[:, t] = moved[:, 2 * width :].astype(BF16).reshape(outer, capacity, width)
        points_out(True, t)

    @pl.loop(0, inner)
    def _(t):
        points_out(False, t)

    arrived[own_outer, own_inner] = outgoing[own_outer, own_inner]
    arrived2[own_outer, own_inner] = outgoing2[own_outer, own_inner]

    mats_out(early)
    mats_out(late)

    def every_other(body):
        @pl.loop(0, owners)
        def _(s):
            @pl.when(s != region)
            def _():
                body(s)

    heads = width // HD
    rows = owners * capacity
    side = width // 2
    near = heads // 2

    def prepare(kind, pairs, empty):
        lane = iota((rows, width), 1)
        marked = jnp.where(lane == side, 1.0, 0.0)
        pairs = jnp.where(empty, 0.0, pairs.astype(F32))
        query = jnp.where(lane < side, pairs, marked)
        queries[kind] = query.astype(BF16).reshape(inner, group, width)
        key = jnp.where(lane < side, pltpu.roll(pairs, side, 1), marked * bias_of(empty))
        keys[kind] = key.astype(BF16).T

    def bias_of(empty):
        return jnp.where(empty, EMPTY_SCORE, 0.0)

    every_other(
        lambda s: points_copy(True, s // inner, lax.rem(s, inner), s, True).wait_recv()
    )
    whole = jnp.concatenate([arrived[:, t].reshape(group, 2 * width) for t in range(inner)], axis=0)
    empty = whole[:, 0:1].astype(F32) == jnp.inf
    prepare(0, whole[:, :width], empty)
    blank[...] = jnp.where(empty, 1.0, 0.0)
    value = whole[:, width:]
    value_lane = iota((rows, width), 1) // HD
    for head in range(heads):
        mask = jnp.where(value_lane == head, 1.0, 0.0).astype(BF16)
        values[head, :, :width] = value * mask
        values[head, :, width:] = mask

    def attend(kind, t):
        query = queries[kind, t]
        lane = iota((group, width), 1)
        total = jnp.zeros((group, 2 * width), F32)
        for head in range(near):
            keep = ((lane // HD) == head) | (lane >= side)
            own = query * jnp.where(keep, 1.0, 0.0).astype(BF16)
            scores = jnp.dot(own, keys[kind], preferred_element_type=F32)
            peak = jnp.max(scores, axis=1, keepdims=True)
            raised = jnp.exp2(scores - peak).astype(BF16)
            total += jnp.dot(raised, values[kind * near + head], preferred_element_type=F32)
        here = (lane // side) == kind
        return jnp.where(here, total[:, :width] / jnp.where(here, total[:, width:], 1.0), 0.0)

    @pl.loop(0, inner)
    def _(t):
        firsts[t] = attend(0, t)

    every_other(
        lambda s: points_copy(False, s // inner, lax.rem(s, inner), s, True).wait_recv()
    )
    prepare(
        1,
        jnp.concatenate([arrived2[:, t].reshape(group, width) for t in range(inner)], axis=0),
        blank[...] > 0,
    )

    def back_copy(a, t, target, arrival):
        other = a * inner + t
        slot = other if arrival else region
        return remote(
            done.at[a, t], returned.at[slot // inner, lax.rem(slot, inner)],
            back_send.at[target], back_recv.at[slot], region=other,
        )

    @pl.loop(0, inner)
    def _(t):
        done[:, t] = (firsts[t] + attend(1, t)).astype(BF16).reshape(outer, capacity, width)

        @pl.loop(0, outer)
        def _(i):
            a = lax.rem(i + own_outer, outer)
            other = a * inner + t

            @pl.when(other != region)
            def _():
                back_copy(a, t, other, False).start()

    returned[own_outer, own_inner] = done[own_outer, own_inner]
    collecting[...] = (iota((points, rows), 1) == column[...]).astype(F32).astype(BF16)

    mats_on(early)
    mats_on(late)

    every_other(lambda s: back_copy(s // inner, lax.rem(s, inner), s, True).wait_recv())

    moved = jnp.dot(
        collecting[...], returned[...].reshape(rows, width), preferred_element_type=F32
    ).astype(BF16)
    share = points // parts
    for part in range(parts):
        held[part] = moved[part * share : (part + 1) * share]

    peers = (twin, across, diagonal)

    def held_copy(i, peer, arrival):
        return remote(
            held.at[peer], att.at[peer if arrival else mine], mp_send.at[i], mp_recv.at[i], mp=peer
        )

    for i, peer in enumerate(peers):
        held_copy(i, peer, False).start()
    att[mine] = held[mine]
    for i in range(4):
        mat(i, twin, 1, twin).wait_recv()
        mat(i, diagonal, 2, twin).wait_recv()
    for i, peer in enumerate(peers):
        held_copy(i, peer, True).wait_recv()

    heads_out = jnp.concatenate([att[i] for i in range(parts)], axis=1)
    own_rows = pl.ds(pl.multiple_of(mine * share, share), share)
    after = (
        cpe[own_rows].astype(F32)
        + jnp.dot(heads_out, projs[...].reshape(points, points), preferred_element_type=F32)
        + bias0[...]
    ).astype(BF16)
    normed = layer_norm(after.astype(F32), g2[...], b2[...]).astype(BF16)
    total = after.astype(F32) + bias2[...]
    wide = fc1s.shape[2]
    for i in range(parts):
        raw = jnp.dot(normed, fc1s[i], preferred_element_type=F32)
        raw += bias1[:, i * wide : (i + 1) * wide]
        hidden = (0.5 * raw * (1.0 + lax.erf(raw * (0.5**0.5)))).astype(BF16)
        total += jnp.dot(hidden, fc2s[i], preferred_element_type=F32)
    final[mine] = total.astype(BF16)

    part_rows = share // 2

    def end_copy(part, piece, slot, peer):
        where = pl.ds(piece * part_rows, part_rows)
        return remote(
            final.at[part, where], final.at[part, where],
            end_send.at[piece, slot], end_recv.at[piece, slot], mp=peer,
        )

    for piece in range(2):
        end_copy(mine, piece, 0, across).start()
    for piece in range(2):
        end_copy(mine, piece, 1, twin).start()
    for piece in range(2):
        end_copy(across, piece, 0, twin).wait_recv()
        end_copy(across, piece, 2, twin).start()

    up.wait_send()
    down.wait_send()
    low_forward(core).wait_send()
    high_forward(core).wait_send()
    for h in range(2):
        for slot in range(3):
            gather_direct(h, twin, slot).wait_send()
    for first in (True, False):
        every_other(
            lambda s: points_copy(first, s // inner, lax.rem(s, inner), s, False).wait_send()
        )
    every_other(lambda s: back_copy(s // inner, lax.rem(s, inner), s, False).wait_send())
    for i in range(4):
        for slot in range(3):
            mat(i, mine, slot, twin).wait_send()
    for i, peer in enumerate(peers):
        held_copy(i, peer, False).wait_send()

    for piece in range(2):
        end_copy(twin, piece, 1, twin).wait_recv()
        end_copy(diagonal, piece, 2, twin).wait_recv()
    for piece in range(2):
        for slot in range(3):
            end_copy(mine, piece, slot, twin).wait_send()
    out_ref[...] = final[...].reshape(out_ref.shape)


def local(
    features, neighbours, order, dest, conv_weight, conv_bias,
    cpe_gain, cpe_shift, norm1_gain, norm1_shift, qkv_weight, proj_weight, proj_bias,
    norm2_gain, norm2_shift, fc1_weight, fc1_bias, fc2_weight, fc2_bias,
):
    points, channels = features.shape
    owners = lax.axis_size("region")
    parts = lax.axis_size("mp")
    capacity = 2 * points // owners
    inner = 4
    outer = owners // inner
    taps, _, width = conv_weight.shape
    rows = owners * capacity
    half = points // 2
    share = points // parts
    heads = width // HD
    wide = fc1_weight.shape[1]
    line = lambda x: x.reshape(1, -1)
    vmem = pl.BlockSpec(memory_space=pltpu.VMEM)
    hbm = pl.BlockSpec(memory_space=pl.ANY)
    blocks = (outer, inner, capacity)
    dma = pltpu.SemaphoreType.DMA
    return pl.pallas_call(
        kernel,
        out_shape=jax.ShapeDtypeStruct(features.shape, BF16),
        in_specs=[
            hbm, vmem, vmem, vmem, hbm, vmem,
            vmem, vmem, vmem, vmem, vmem, hbm, vmem, vmem, vmem, hbm, vmem, hbm, vmem,
        ],
        out_specs=vmem,
        scratch_shapes=[
            pltpu.VMEM((points + 2 * RIM, channels), BF16),
            pltpu.VMEM((points, LANES), jnp.int32),
            pltpu.VMEM((points, width), F32),
            pltpu.VMEM((points, TAPS * width), BF16),
            pltpu.VMEM((taps, channels, width), BF16),
            pltpu.VMEM((parts, 2, half, width), BF16),
            pltpu.VMEM((points, channels), BF16),
            pltpu.VMEM((points, 3 * width), BF16),
            pltpu.VMEM((points, 1), jnp.int32),
            pltpu.VMEM((1, points), jnp.int32),
            pltpu.VMEM(blocks + (2 * width,), BF16),
            pltpu.VMEM(blocks + (2 * width,), BF16),
            pltpu.VMEM(blocks + (width,), BF16),
            pltpu.VMEM(blocks + (width,), BF16),
            pltpu.VMEM((2, inner, outer * capacity, width), BF16),
            pltpu.VMEM((2, width, rows), BF16),
            pltpu.VMEM((heads, rows, 2 * width), BF16),
            pltpu.VMEM((inner, outer * capacity, width), F32),
            pltpu.VMEM((rows, 1), F32),
            pltpu.VMEM((points, rows), BF16),
            pltpu.VMEM(blocks + (width,), BF16),
            pltpu.VMEM(blocks + (width,), BF16),
            pltpu.VMEM((parts, share, width), BF16),
            pltpu.VMEM((parts, share, width), BF16),
            pltpu.VMEM((parts, share, channels), BF16),
            pltpu.VMEM((parts,) + proj_weight.shape, BF16),
            pltpu.VMEM((parts,) + fc1_weight.shape, BF16),
            pltpu.VMEM((parts,) + fc2_weight.shape, BF16),
            dma((4,)), dma((taps // TAPS,)), dma((4,)), dma((4,)), dma((2, 3)), dma((2, 3)),
            dma((2, owners)), dma((2, owners)), dma((owners,)), dma((owners,)), dma((3,)), dma((3,)),
            dma((2, 3)), dma((2, 3)), dma((4, 3)), dma((4, 3)),
        ],
        compiler_params=pltpu.CompilerParams(
            collective_id=0, has_side_effects=True, vmem_limit_bytes=VMEM_LIMIT
        ),
        name="block",
    )(
        features, neighbours.T, order, dest.T, conv_weight, line(conv_bias),
        line(cpe_gain), line(cpe_shift), line(norm1_gain), line(norm1_shift), qkv_weight,
        proj_weight, line(proj_bias), line(norm2_gain), line(norm2_shift),
        fc1_weight, line(fc1_bias), fc2_weight, line(fc2_bias),
    )


def solution(mesh):
    row = P("region", None)
    placed = (
        row, row, row, row, P(None, None, "mp"), P("mp"),
        P(), P(), P(), P(), P(None, None, "mp"), P("mp", None), P(),
        P(), P(), P(None, "mp"), P(), P("mp", None), P(),
    )
    return jax.shard_map(
        local, mesh=mesh, in_specs=placed, out_specs=P("region", None), check_vma=False
    )
```
